32 devices in a mesh: clips: 2 (over y), video: 4 (over z), audio: 4 (over x, core).
Axes of the slice: x: 2, y: 2, z: 4, core: 2. Of those that a mesh axis runs over, the one named last changes fastest.
Arguments:
- video_q: bfloat16 [5120, 1536], P(('clips', 'video', 'audio')), parts along dimension 0, may hold values from -130 to 130
- video_k: bfloat16 [5120, 1536], P(('clips', 'video', 'audio')), parts along dimension 0, may hold values from -130 to 130
- video_v: bfloat16 [5120, 1536], P(('clips', 'video', 'audio')), parts along dimension 0, may hold values from -6 to 6
- audio_q: bfloat16 [512, 1536], P(('clips', 'video', 'audio')), parts along dimension 0, may hold values from -130 to 130
- audio_k: bfloat16 [512, 1536], P(('clips', 'video', 'audio')), parts along dimension 0, may hold values from -130 to 130
- audio_v: bfloat16 [512, 1536], P(('clips', 'video', 'audio')), parts along dimension 0, may hold values from -6 to 6
- norm_gain: float32 [4, 1536], replicated, may hold values from 0.49 to 6
- video_dout: bfloat16 [5120, 1536], P(('clips', 'video', 'audio')), parts along dimension 0, may hold values from -6 to 6
- audio_dout: bfloat16 [512, 1536], P(('clips', 'video', 'audio')), parts along dimension 0, may hold values from -6 to 6
- link: int32 [32, 5], P(('clips', 'video', 'audio')), parts along dimension 0, may hold values from 0 to 1, as said below
Outputs:
- video_out: bfloat16 [5120, 1536], P(('clips', 'video', 'audio')), parts along dimension 0
- audio_out: bfloat16 [512, 1536], P(('clips', 'video', 'audio')), parts along dimension 0
- grad_video_q: bfloat16 [5120, 1536], P(('clips', 'video', 'audio')), parts along dimension 0
- grad_video_k: bfloat16 [5120, 1536], P(('clips', 'video', 'audio')), parts along dimension 0
- grad_video_v: bfloat16 [5120, 1536], P(('clips', 'video', 'audio')), parts along dimension 0
- grad_audio_q: bfloat16 [512, 1536], P(('clips', 'video', 'audio')), parts along dimension 0
- grad_audio_k: bfloat16 [512, 1536], P(('clips', 'video', 'audio')), parts along dimension 0
- grad_audio_v: bfloat16 [512, 1536], P(('clips', 'video', 'audio')), parts along dimension 0
The draws below stay inside these ranges and needn't reach their ends.
There are 2 independent parts, one for each index of `clips`. The reference program is written for one: setup_inputs(seed, part) draws one part's arguments, and reference() takes and returns one part's arrays. A program takes and returns all parts, laid end to end along the dimension named above; an argument that names none is the same for every part. Nothing has to cross between parts.
Inputs may be any that keep to these rules, and one draw needn't show every extreme that they name: `link`: row b, column j links video block b with audio block b + j - 2; column 2 is 1 in every row, the ones of a row are consecutive, and columns that name an audio block outside 0 to 15 are 0.
All inputs are finite; a program needn't handle non-finite values.
Results may differ from the reference program's by a relative error of at most 0.038.
The reference program's roundings to bfloat16 on the way count: a program that leaves them out, or rounds other values in their place, can miss the bound.
Values may be sent and summed in bfloat16 or wider, within the bound.
A program may use at most 64 MiB of HBM per device.

```python
import math
import jax
import jax.numpy as jnp
from jax import lax

H = 12
DH = 128
HD = 1536
VT_DEV = 160
AT_DEV = 16
FRAME = 960
AFRAME = 96
R = 2
SPAN = 5
NBLK = 16
VTOK = 2560
ATOK = 256


def rough_rows(key, row_count):
    key_list = jax.random.split(key, 5)
    normal_part = jnp.clip(jax.random.normal(key_list[0], (row_count, HD), jnp.float32), -4.0, 4.0)
    row_scale = jnp.exp(jax.random.uniform(key_list[3], (row_count, 1), jnp.float32, 0.0, 2.3))
    column_scale = jnp.exp(jax.random.uniform(key_list[4], (1, HD), jnp.float32, 0.0, 2.3))
    blended = normal_part
    return blended * row_scale * column_scale / 10.0


def twin_field(key, salt, row_count, first_row, frame_rows):
    base_rows = rough_rows(jax.random.fold_in(key, salt), row_count)
    frame_count = VTOK // FRAME
    anchors = jnp.arange(frame_count) * frame_rows + first_row
    return base_rows.at[anchors + 1].set(base_rows[anchors + 1])


def draw_audio_k(key, part):
    return twin_field(key, 11, ATOK, 0, AFRAME).astype(jnp.bfloat16)


def draw_video_k(key, part):
    return twin_field(key, 31, VTOK, 1, FRAME).astype(jnp.bfloat16)


def draw_video_q(key, part):
    own_key = jax.random.fold_in(key, 21)
    return rough_rows(own_key, VTOK).astype(jnp.bfloat16)


def draw_audio_q(key, part):
    own_key = jax.random.fold_in(key, 41)
    return rough_rows(own_key, ATOK).astype(jnp.bfloat16)


def draw_norm_gain(key, part):
    key = jax.random.fold_in(key, 5)
    return jnp.exp(jax.random.uniform(key, (4, HD), jnp.float32, -0.69, 0.69))


def draw_link(key, part):
    key = jax.random.fold_in(key, 7)
    key_list = jax.random.split(key, 3)
    reach_low = jnp.clip(jax.random.randint(key_list[0], (NBLK,), 0, 2 * R + 1) - R, 0, R)
    reach_high = jnp.clip(jax.random.randint(key_list[1], (NBLK,), 0, 2 * R + 1) - R, 0, R)
    widest = jax.random.randint(key_list[2], (), R, NBLK - R)
    blocks = jnp.arange(NBLK)
    reach_low = jnp.where(blocks == widest, R, reach_low)
    reach_high = jnp.where(blocks == widest, R, reach_high)
    offsets = jnp.arange(SPAN) - R
    linked_cols = (offsets[None, :] >= -reach_low[:, None]) & (offsets[None, :] <= reach_high[:, None])
    target = blocks[:, None] + offsets[None, :]
    inside = (target >= 0) & (target < NBLK)
    return (linked_cols & inside).astype(jnp.int32)


def levels(key, extent, pieces, smallest, top_value):
    gain, own = 1.0, jax.random.fold_in(key, 6)
    for position, blocks in pieces:
        draws = jnp.exp(jax.random.uniform(jax.random.fold_in(own, position), (blocks,), jnp.float32, smallest / len(pieces), top_value / len(pieces)))
        gain = gain * jnp.repeat(draws, extent[position] // blocks).reshape([-1 if axis == position else 1 for axis in range(len(extent))])
    return gain


def centred(rng, dims, scale, bound, shards=(), kind=jnp.bfloat16):
    factor_of = levels(rng, dims, shards, -0.22, 0.18) if shards else 1.0
    values = jax.random.normal(rng, dims, jnp.float32) * scale * factor_of
    return jnp.minimum(jnp.maximum(values, -bound), bound).astype(kind)


def setup_inputs(seed: int = 0, part: int = 0) -> dict:
    keys = jax.random.split(jax.random.key(seed), 11)
    part_splits = jax.random.split(jax.random.fold_in(keys[10], part), 11)
    return {
        "video_q": draw_video_q(jax.random.fold_in(jax.random.fold_in(keys[10], part), 71), part),
        "video_k": draw_video_k(jax.random.fold_in(jax.random.fold_in(keys[10], part), 71), part),
        "video_v": centred(part_splits[2], (VTOK, HD), 1.0, 6.0, ((0, 16),)),
        "audio_q": draw_audio_q(jax.random.fold_in(jax.random.fold_in(keys[10], part), 71), part),
        "audio_k": draw_audio_k(jax.random.fold_in(jax.random.fold_in(keys[10], part), 71), part),
        "audio_v": centred(part_splits[5], (ATOK, HD), 1.0, 6.0, ((0, 16),)),
        "norm_gain": draw_norm_gain(jax.random.fold_in(keys[10], 71), part),
        "video_dout": centred(part_splits[7], (VTOK, HD), 1.0, 6.0, ((0, 16),)),
        "audio_dout": centred(part_splits[8], (ATOK, HD), 1.0, 6.0, ((0, 16),)),
        "link": draw_link(jax.random.fold_in(jax.random.fold_in(keys[10], part), 71), part),
    }


EPSILON = 1e-06
HUGE = 1e+30

def prepare(values, gain_row, places):
    row_count = values.shape[0]
    head_count = values.shape[1] // DH
    half_size = DH // 2
    shaped = values.reshape(row_count, head_count, DH)
    scaled = shaped * lax.rsqrt(lax.optimization_barrier(jnp.mean(shaped * shaped, axis=-1, keepdims=True)) + EPSILON)
    normed = scaled * gain_row.reshape(head_count, DH)
    inverse = jnp.exp(jnp.arange(half_size).astype(jnp.float32) * (-2.0 * math.log(10000.0) / DH))
    angles = places[:, None] * inverse[None, :]
    cosine = jnp.cos(angles)[:, None, :]
    sine_part = jnp.sin(angles)[:, None, :]
    first_half = normed[:, :, :half_size]
    second_half = normed[:, :, half_size:]
    turned = jnp.concatenate([first_half * cosine - second_half * sine_part, second_half * cosine + first_half * sine_part], axis=-1)
    return turned.reshape(row_count, head_count * DH)

def rounded(values):
    return lax.optimization_barrier(values.astype(jnp.bfloat16)).astype(jnp.float32)

def widened(values):
    return values.astype(jnp.float32)

def reference(video_q, video_k, video_v, audio_q, audio_k, audio_v, norm_gain, video_dout, audio_dout, link):
    attn_scale = DH ** (-0.5)
    video_places = (jnp.arange(VTOK) // FRAME).astype(jnp.float32)
    audio_places = jnp.arange(ATOK).astype(jnp.float32) / AFRAME
    query_video, query_video_back = jax.vjp(lambda values: prepare(values, norm_gain[0], video_places), widened(video_q))
    key_video, key_video_back = jax.vjp(lambda values: prepare(values, norm_gain[1], video_places), widened(video_k))
    query_audio, query_audio_back = jax.vjp(lambda values: prepare(values, norm_gain[2], audio_places), widened(audio_q))
    key_audio, key_audio_back = jax.vjp(lambda values: prepare(values, norm_gain[3], audio_places), widened(audio_k))
    block_shape = (NBLK, VT_DEV, H, DH)
    video_qr = query_video.astype(jnp.bfloat16).reshape(block_shape)
    video_kr = key_video.astype(jnp.bfloat16).reshape(block_shape)
    video_vr = video_v.reshape(block_shape)
    video_gr = video_dout.reshape(block_shape)
    pad_rows = R * AT_DEV
    window_rows = SPAN * AT_DEV

    def padded(values):
        return jnp.pad(values, ((pad_rows, pad_rows), (0, 0)))
    audio_qp = padded(query_audio.astype(jnp.bfloat16)).reshape(-1, H, DH)
    audio_kp = padded(key_audio.astype(jnp.bfloat16)).reshape(-1, H, DH)
    audio_vp = padded(audio_v).reshape(-1, H, DH)

    def video_side(block_index):
        start_row = block_index * AT_DEV
        key_win = lax.dynamic_slice_in_dim(audio_kp, start_row, window_rows, 0)
        value_win = lax.dynamic_slice_in_dim(audio_vp, start_row, window_rows, 0)
        keep_rows = jnp.repeat(link[block_index] > 0, AT_DEV)
        scores = jnp.einsum('qhd,khd->hqk', widened(video_qr[block_index]), widened(key_win)) * attn_scale
        masked = jnp.where(keep_rows[None, None, :], scores, -HUGE)
        return (masked, key_win, value_win, keep_rows)

    def forward_block(block_index):
        masked, key_win, value_win, keep_rows = video_side(block_index)
        top_score = lax.optimization_barrier(jnp.max(masked, axis=-1))
        weights = jnp.exp(masked - top_score[:, :, None])
        total_sum = lax.optimization_barrier(jnp.sum(weights, axis=-1))
        mixed_sum = jnp.einsum('hqk,khd->qhd', rounded(weights), widened(value_win))
        out_block = (mixed_sum / total_sum.T[:, :, None]).astype(jnp.bfloat16)
        lse_block = top_score + jnp.log(total_sum)
        query_win = lax.dynamic_slice_in_dim(audio_qp, block_index * AT_DEV, window_rows, 0)
        scores_a = jnp.einsum('ahd,khd->hak', widened(query_win), widened(video_kr[block_index])) * attn_scale
        top_a = lax.optimization_barrier(jnp.max(scores_a, axis=-1))
        weights_a = jnp.exp(scores_a - top_a[:, :, None])
        total_a = lax.optimization_barrier(jnp.sum(weights_a, axis=-1))
        mixed_a = jnp.einsum('hak,khd->ahd', rounded(weights_a), widened(video_vr[block_index])).astype(jnp.bfloat16)
        mixed_a = jnp.where(keep_rows[:, None, None], mixed_a, jnp.zeros_like(mixed_a))
        top_a = jnp.where(keep_rows[:, None], top_a.T, 0.0)
        total_a = jnp.where(keep_rows[:, None], total_a.T, 0.0)
        return (out_block, lse_block, mixed_a, top_a, total_a)
    block_ids = jnp.arange(NBLK, dtype=jnp.int32)
    out_all, lse_all, part_mixed, part_top, part_total = lax.map(forward_block, block_ids)

    def align_slots(stacked):
        shaped = stacked.reshape((NBLK, SPAN, AT_DEV) + stacked.shape[2:])
        padded_blocks = jnp.pad(shaped, [(R, R)] + [(0, 0)] * (shaped.ndim - 1))
        return jnp.stack([padded_blocks[2 * R - slot_index:2 * R - slot_index + NBLK, slot_index] for slot_index in range(SPAN)])
    stack_mixed = align_slots(part_mixed)
    stack_top = align_slots(part_top)
    stack_total = align_slots(part_total)
    valid_parts = stack_total > 0.0
    lifted = jnp.where(valid_parts, stack_top, -HUGE)
    best_top = lax.optimization_barrier(jnp.max(lifted, axis=0))
    factors = jnp.where(valid_parts, jnp.exp(lifted - best_top[None]), 0.0)
    total_audio = lax.optimization_barrier(jnp.sum(factors * stack_total, axis=0))
    combined = lax.optimization_barrier(jnp.sum(factors[..., None] * widened(stack_mixed), axis=0)) / total_audio[..., None]
    audio_out = combined.astype(jnp.bfloat16).reshape(ATOK, H, DH)
    lse_audio = (best_top + jnp.log(total_audio)).reshape(ATOK, H)
    audio_gr = audio_dout.reshape(ATOK, H, DH)
    delta_audio = lax.optimization_barrier(jnp.sum(widened(audio_gr) * widened(audio_out), axis=-1))
    grad_audio_p = padded(audio_dout).reshape(-1, H, DH)
    lse_p = padded(lse_audio)
    delta_p = padded(delta_audio)

    def backward_block(block_index):
        masked, key_win, value_win, keep_rows = video_side(block_index)
        grad_rows = video_gr[block_index]
        probs_v = jnp.exp(masked - lse_all[block_index][:, :, None])
        dvalue_win = jnp.einsum('hqk,qhd->khd', rounded(probs_v), widened(grad_rows)).astype(jnp.bfloat16)
        dprob_v = jnp.einsum('qhd,khd->hqk', widened(grad_rows), widened(value_win))
        delta_video = lax.optimization_barrier(jnp.sum(widened(grad_rows) * widened(out_all[block_index]), axis=-1)).T
        dscore_v = rounded(probs_v * (dprob_v - delta_video[:, :, None]))
        dquery_video = jnp.einsum('hqk,khd->qhd', dscore_v, widened(key_win)) * attn_scale
        dkey_win = (jnp.einsum('hqk,qhd->khd', dscore_v, widened(video_qr[block_index])) * attn_scale).astype(jnp.bfloat16)
        start_row = block_index * AT_DEV
        query_win = lax.dynamic_slice_in_dim(audio_qp, start_row, window_rows, 0)
        grad_win = lax.dynamic_slice_in_dim(grad_audio_p, start_row, window_rows, 0)
        lse_win = lax.dynamic_slice_in_dim(lse_p, start_row, window_rows, 0)
        delta_win = lax.dynamic_slice_in_dim(delta_p, start_row, window_rows, 0)
        scores_a = jnp.einsum('ahd,khd->hak', widened(query_win), widened(video_kr[block_index])) * attn_scale
        probs_a = jnp.where(keep_rows[None, :, None], jnp.exp(scores_a - lse_win.T[:, :, None]), 0.0)
        dvalue_video = jnp.einsum('hak,ahd->khd', rounded(probs_a), widened(grad_win))
        dprob_a = jnp.einsum('ahd,khd->hak', widened(grad_win), widened(video_vr[block_index]))
        dscore_a = rounded(probs_a * (dprob_a - delta_win.T[:, :, None]))
        dkey_video = jnp.einsum('hak,ahd->khd', dscore_a, widened(query_win)) * attn_scale
        dquery_win = (jnp.einsum('hak,khd->ahd', dscore_a, widened(video_kr[block_index])) * attn_scale).astype(jnp.bfloat16)
        return (dquery_video, dkey_video, dvalue_video, dkey_win, dvalue_win, dquery_win)
    dq_video, dk_video, dv_video, dk_window, dv_window, dq_window = lax.map(backward_block, block_ids)
    channels = H * DH
    dq_audio = lax.optimization_barrier(jnp.sum(widened(align_slots(dq_window)), axis=0)).reshape(ATOK, channels)
    dk_audio = lax.optimization_barrier(jnp.sum(widened(align_slots(dk_window)), axis=0)).reshape(ATOK, channels)
    dv_audio = lax.optimization_barrier(jnp.sum(widened(align_slots(dv_window)), axis=0)).reshape(ATOK, channels)
    grad_video_q = query_video_back(dq_video.reshape(VTOK, channels))[0].astype(jnp.bfloat16)
    grad_video_k = key_video_back(dk_video.reshape(VTOK, channels))[0].astype(jnp.bfloat16)
    grad_video_v = dv_video.reshape(VTOK, channels).astype(jnp.bfloat16)
    grad_audio_q = query_audio_back(dq_audio)[0].astype(jnp.bfloat16)
    grad_audio_k = key_audio_back(dk_audio)[0].astype(jnp.bfloat16)
    grad_audio_v = dv_audio.astype(jnp.bfloat16)
    return (out_all.reshape(VTOK, channels), audio_out.reshape(ATOK, channels), grad_video_q, grad_video_k, grad_video_v, grad_audio_q, grad_audio_k, grad_audio_v)
```

```python
import functools
import math

import jax
import jax.numpy as jnp
from jax import lax
from jax.experimental import pallas as pl
from jax.experimental.pallas import tpu as pltpu
from jax.sharding import PartitionSpec as P

DH = 128
FRAME = 960
AFRAME = 96
R = 2
SPAN = 5
EPSILON = 1e-06
HUGE = 1e30
SCALE = DH ** (-0.5)
SLOTS = (0, 1, 3, 4)
REACH = 2 * R
AUDIO_Q, AUDIO_DOUT, AUDIO_K, AUDIO_V = range(4)
D_KEY, D_VALUE, D_QUERY = range(3)
f32 = jnp.float32
bf16 = jnp.bfloat16


def nt(a, b):
    return lax.dot_general(a, b, (((1,), (1,)), ((), ())), preferred_element_type=f32)


def nn(a, b):
    return lax.dot_general(a, b, (((1,), (0,)), ((), ())), preferred_element_type=f32)


def tn(a, b):
    return lax.dot_general(a, b, (((0,), (0,)), ((), ())), preferred_element_type=f32)


def swapped(x):
    return pltpu.roll(x, DH // 2, 1)


def rinv_of(x):
    return lax.rsqrt(jnp.mean(x * x, axis=-1, keepdims=True) + EPSILON)


def turn(x, rinv, gain, cosine, sine):
    n = x * rinv * gain
    return n * cosine + swapped(n) * sine


def turn_back(dy, x, rinv, gain, cosine, sine):
    dn = dy * cosine - swapped(dy) * sine
    hat = x * rinv
    dh = dn * gain
    return rinv * (dh - hat * jnp.mean(dh * hat, axis=-1, keepdims=True))


def tables(places):
    lane = lax.broadcasted_iota(jnp.int32, places.shape, 1)
    half = DH // 2
    channel = jnp.where(lane < half, lane, lane - half).astype(f32)
    angles = places * jnp.exp(channel * (-2.0 * math.log(10000.0) / DH))
    sine = jnp.sin(angles)
    return jnp.cos(angles), jnp.where(lane < half, -sine, sine)


def kernel(
    along, count, vq, vk, vv, aq, ak, av, gain, vdo, ado, link,
    o_v, o_a, g_vq, g_vk, g_vv, g_aq, g_ak, g_av,
    win, po, po_in, gr, gr_in, stat, qv, kv, ea, dpa, pab, gab, rq, rk, tab_v, tab_a, coef, bias, wts,
    s_win, r_win, s_stat, r_stat, s_po, r_po, s_gr, r_gr,
):
    vrows, hd = vq.shape
    arows = aq.shape[0]
    heads = hd // DH
    wrows = SPAN * arows
    clip = lax.axis_index("clips")
    me = lax.axis_index("video") * along + lax.axis_index("audio")

    def valid(i):
        return jnp.logical_and(i >= 0, i < count)

    def device(i):
        return (clip, i // along, lax.rem(i, along))

    def rows(j):
        return pl.ds(j * arows, arows)

    def lanes(h):
        return pl.ds(pl.multiple_of(h * DH, DH), DH)

    others = [d for d in range(-REACH, REACH + 1) if d]

    barrier = pltpu.get_barrier_semaphore()
    for d in others:

        @pl.when(valid(me + d))
        def _():
            pl.semaphore_signal(
                barrier, inc=1, device_id=device(me + d), device_id_type=pl.DeviceIdType.MESH
            )

    row = lax.broadcasted_iota(jnp.int32, (arows, DH), 0)
    c, s = tables((me * arows + row).astype(f32) / AFRAME)
    tab_a[0], tab_a[1] = c, s
    vplace = jnp.zeros((8, DH), jnp.int32) + (me * vrows) // FRAME
    c, s = tables(vplace.astype(f32))
    tab_v[0], tab_v[1] = c, s

    def audio_prepare(h, _):
        hs = lanes(h)
        for src, slot, g in ((aq, AUDIO_Q, 2), (ak, AUDIO_K, 3)):
            x = src[:, hs].astype(f32)
            y = turn(x, rinv_of(x), gain[g : g + 1, hs], tab_a[0], tab_a[1])
            win[slot, rows(R), hs] = y.astype(bf16)
        return 0

    lax.fori_loop(0, heads, audio_prepare, 0)
    win[AUDIO_DOUT, rows(R), :] = ado[...]
    win[AUDIO_V, rows(R), :] = av[...]

    pl.semaphore_wait(barrier, jnp.minimum(me, REACH) + jnp.minimum(count - 1 - me, REACH))

    def win_copy(member, n, to):
        j = SLOTS[n]
        return pltpu.make_async_remote_copy(
            src_ref=win.at[member, rows(R)],
            dst_ref=win.at[member, rows(j)],
            send_sem=s_win.at[member, n],
            recv_sem=r_win.at[member, n],
            device_id=device(to),
            device_id_type=pl.DeviceIdType.MESH,
        )

    def back_copy(src, dst, send, recv, n, to):
        j = SLOTS[n]
        return pltpu.make_async_remote_copy(
            src_ref=src.at[rows(j)],
            dst_ref=dst.at[rows(j)],
            send_sem=send.at[n],
            recv_sem=recv.at[n],
            device_id=device(to),
            device_id_type=pl.DeviceIdType.MESH,
        )

    def stat_copy(d, to):
        n = others.index(d)
        return pltpu.make_async_remote_copy(
            src_ref=stat.at[REACH],
            dst_ref=stat.at[REACH - d],
            send_sem=s_stat.at[n],
            recv_sem=r_stat.at[n],
            device_id=device(to),
            device_id_type=pl.DeviceIdType.MESH,
        )

    def win_each(members, action):
        for member in members:
            for n, j in enumerate(SLOTS):
                other = me + j - R if action == "wait_recv" else me + R - j

                @pl.when(valid(other))
                def _():
                    getattr(win_copy(member, n, other), action)()

    def back_each(src, dst, send, recv, action):
        for n, j in enumerate(SLOTS):
            other = me + R - j if action == "wait_recv" else me + j - R

            @pl.when(valid(other))
            def _():
                getattr(back_copy(src, dst, send, recv, n, other), action)()

    def stat_each(action):
        for d in others:
            other = me - d if action == "wait_recv" else me + d

            @pl.when(valid(other))
            def _():
                getattr(stat_copy(d, other), action)()

    win_each((AUDIO_Q, AUDIO_DOUT, AUDIO_K, AUDIO_V), "start")

    for j in SLOTS:

        @pl.when(jnp.logical_not(valid(me + j - R)))
        def _():
            for member in range(4):
                win[member, rows(j), :] = jnp.zeros((arows, hd), bf16)

        @pl.when(jnp.logical_not(valid(me + R - j)))
        def _():
            po_in[rows(j), :] = jnp.zeros((arows, hd), bf16)
            for member in range(3):
                gr_in[member, rows(j), :] = jnp.zeros((arows, hd), bf16)

    empty = jnp.where(lax.broadcasted_iota(jnp.int32, (48, DH), 0) < 16, -HUGE, 0.0)
    stat[REACH] = empty
    for d in others:

        @pl.when(jnp.logical_not(valid(me - d)))
        def _():
            stat[REACH - d] = empty

    lane_slot = lax.broadcasted_iota(jnp.int32, (1, wrows), 1) // arows
    linked_row = jnp.zeros((1, wrows), jnp.int32)
    for j in range(SPAN):
        on = link[0, j]
        bias[rows(j), :] = jnp.zeros((arows, vrows), f32) + jnp.where(on > 0, 0.0, -HUGE)
        linked_row = jnp.where(lane_slot == j, on, linked_row)
    linked_row = linked_row > 0

    def video_prepare(h, _):
        hs = lanes(h)
        for src, dst, keep, g in ((vq, qv, rq, 0), (vk, kv, rk, 1)):
            x = src[:, hs].astype(f32)
            rinv = rinv_of(x)
            keep[:, hs] = jnp.broadcast_to(rinv, (vrows, DH))
            y = turn(x, rinv, gain[g : g + 1, hs], tab_v[0, 0:1], tab_v[1, 0:1])
            dst[:, hs] = y.astype(bf16)
        return 0

    lax.fori_loop(0, heads, video_prepare, 0)

    win_each((AUDIO_Q, AUDIO_DOUT), "wait_recv")

    def audio_forward(h, _):
        hs = lanes(h)
        v = vv[:, hs]
        r = nt(kv[:, hs], win[AUDIO_Q, :, hs]) * SCALE
        top = jnp.max(r, axis=0, keepdims=True)
        e = jnp.exp(r - top)
        ea[h] = e
        dp = nt(v, win[AUDIO_DOUT, :, hs])
        dpa[h] = dp
        stat[REACH, pl.ds(h, 1), 0:wrows] = jnp.where(linked_row, top, -HUGE)
        stat[REACH, pl.ds(16 + h, 1), 0:wrows] = jnp.where(
            linked_row, jnp.sum(e, axis=0, keepdims=True), 0.0
        )
        stat[REACH, pl.ds(32 + h, 1), 0:wrows] = jnp.where(
            linked_row, jnp.sum(e * dp, axis=0, keepdims=True), 0.0
        )
        po[:, hs] = tn(e.astype(bf16), v).astype(bf16)
        return 0

    lax.fori_loop(0, heads, audio_forward, 0)
    stat_each("start")
    back_each(po, po_in, s_po, r_po, "start")

    win_each((AUDIO_K, AUDIO_V), "wait_recv")

    def video_side(h, _):
        hs = lanes(h)
        ka, va = win[AUDIO_K, :, hs], win[AUDIO_V, :, hs]
        q, do = qv[:, hs], vdo[:, hs]
        sc = nt(ka, q) * SCALE + bias[...]
        top = jnp.max(sc, axis=0, keepdims=True)
        e = jnp.exp(sc - top)
        p = e * (1.0 / jnp.sum(e, axis=0, keepdims=True))
        pb = p.astype(bf16)
        o_v[:, hs] = tn(pb, va).astype(bf16)
        dp = nt(va, do)
        delta = jnp.sum(p * dp, axis=0, keepdims=True)
        gs = (p * (dp - delta)).astype(bf16)
        gr[D_KEY, :, hs] = (nn(gs, q) * SCALE).astype(bf16)
        gr[D_VALUE, :, hs] = nn(pb, do).astype(bf16)
        dq = tn(gs, ka) * SCALE
        g_vq[:, hs] = turn_back(
            dq, vq[:, hs].astype(f32), rq[:, hs], gain[0:1, hs], tab_v[0, 0:1], tab_v[1, 0:1]
        ).astype(bf16)
        return 0

    lax.fori_loop(0, heads, video_side, 0)
    for member in (D_KEY, D_VALUE):
        back_each(gr.at[member], gr_in.at[member], s_gr.at[member], r_gr.at[member], "start")

    stat_each("wait_recv")
    lane = lax.broadcasted_iota(jnp.int32, (16, DH), 1)
    tops, totals, dots = [], [], []
    for t in range(2 * REACH + 1):
        shift = (t - REACH) * arows
        inside = jnp.logical_and(lane >= shift, lane < shift + wrows)
        rolled = [
            pltpu.roll(stat[t, 16 * i : 16 * i + 16], shift % DH, 1) if shift else stat[t, 16 * i : 16 * i + 16]
            for i in range(3)
        ]
        tops.append(jnp.where(inside, rolled[0], -HUGE))
        totals.append(jnp.where(inside, rolled[1], 0.0))
        dots.append(jnp.where(inside, rolled[2], 0.0))
    best = functools.reduce(jnp.maximum, tops)
    factors = [jnp.where(a > -0.5 * HUGE, jnp.exp(a - best), 0.0) for a in tops]
    total = sum(a * b for a, b in zip(factors, totals))
    inverse = 1.0 / jnp.where(total > 0.0, total, 1.0)
    coef[0] = factors[REACH] * inverse
    coef[1] = sum(a * b for a, b in zip(factors, dots)) * inverse
    wts[...] = jnp.zeros(wts.shape, f32)
    for j in range(SPAN):
        wts[16 * j : 16 * j + 16, :] = factors[REACH + R - j] * inverse

    def audio_back(h, _):
        hs = lanes(h)
        p = ea[h] * coef[0, pl.ds(h, 1), 0:wrows]
        ga = (p * (dpa[h] - coef[1, pl.ds(h, 1), 0:wrows])).astype(bf16)
        pab[h] = p.astype(bf16)
        gab[h] = ga
        gr[D_QUERY, :, hs] = (tn(ga, kv[:, hs]) * SCALE).astype(bf16)
        return 0

    lax.fori_loop(0, heads, audio_back, 0)
    back_each(gr.at[D_QUERY], gr_in.at[D_QUERY], s_gr.at[D_QUERY], r_gr.at[D_QUERY], "start")

    def video_back(h, _):
        hs = lanes(h)
        g_vv[:, hs] = nn(pab[h], win[AUDIO_DOUT, :, hs]).astype(bf16)
        dk = nn(gab[h], win[AUDIO_Q, :, hs]) * SCALE
        g_vk[:, hs] = turn_back(
            dk, vk[:, hs].astype(f32), rk[:, hs], gain[1:2, hs], tab_v[0, 0:1], tab_v[1, 0:1]
        ).astype(bf16)
        return 0

    lax.fori_loop(0, heads, video_back, 0)

    turned = jnp.transpose(wts[...])[R * arows : (R + 1) * arows, :]
    back_each(po, po_in, s_po, r_po, "wait_recv")
    for h in range(heads):
        hs = slice(h * DH, (h + 1) * DH)
        acc = jnp.zeros((arows, DH), f32)
        for j in range(SPAN):
            part = (po if j == R else po_in)[j * arows : (j + 1) * arows, hs].astype(f32)
            acc += turned[:, 16 * j + h : 16 * j + h + 1] * part
        o_a[:, hs] = acc.astype(bf16)

    def merged(member, hs):
        acc = gr[member, rows(R), hs].astype(f32)
        for j in SLOTS:
            acc += gr_in[member, rows(j), hs].astype(f32)
        return acc

    def audio_grad(src, member, g, dst):
        def body(h, _):
            hs = lanes(h)
            x = src[:, hs].astype(f32)
            dst[:, hs] = turn_back(
                merged(member, hs), x, rinv_of(x), gain[g : g + 1, hs], tab_a[0], tab_a[1]
            ).astype(bf16)
            return 0

        lax.fori_loop(0, heads, body, 0)

    for member in (D_KEY, D_VALUE):
        back_each(gr.at[member], gr_in.at[member], s_gr.at[member], r_gr.at[member], "wait_recv")
    g_av[...] = merged(D_VALUE, slice(None)).astype(bf16)
    audio_grad(ak, D_KEY, 3, g_ak)
    back_each(gr.at[D_QUERY], gr_in.at[D_QUERY], s_gr.at[D_QUERY], r_gr.at[D_QUERY], "wait_recv")
    audio_grad(aq, D_QUERY, 2, g_aq)

    win_each(range(4), "wait_send")
    stat_each("wait_send")
    back_each(po, po_in, s_po, r_po, "wait_send")
    for member in range(3):
        back_each(gr.at[member], gr_in.at[member], s_gr.at[member], r_gr.at[member], "wait_send")


def on_device(along, count, *args):
    vq, aq = args[0], args[3]
    vrows, hd = vq.shape
    arows = aq.shape[0]
    heads = hd // DH
    wrows = SPAN * arows
    video = jax.ShapeDtypeStruct((vrows, hd), bf16)
    audio = jax.ShapeDtypeStruct((arows, hd), bf16)
    vmem = pl.BlockSpec(memory_space=pltpu.VMEM)
    dma = pltpu.SemaphoreType.DMA
    n = len(SLOTS)
    scratch = [
        pltpu.VMEM((4, wrows, hd), bf16),
        pltpu.VMEM((wrows, hd), bf16),
        pltpu.VMEM((wrows, hd), bf16),
        pltpu.VMEM((3, wrows, hd), bf16),
        pltpu.VMEM((3, wrows, hd), bf16),
        pltpu.VMEM((2 * REACH + 1, 48, DH), f32),
        pltpu.VMEM((vrows, hd), bf16),
        pltpu.VMEM((vrows, hd), bf16),
        pltpu.VMEM((heads, vrows, wrows), f32),
        pltpu.VMEM((heads, vrows, wrows), f32),
        pltpu.VMEM((heads, vrows, wrows), bf16),
        pltpu.VMEM((heads, vrows, wrows), bf16),
        pltpu.VMEM((vrows, hd), f32),
        pltpu.VMEM((vrows, hd), f32),
        pltpu.VMEM((2, 8, DH), f32),
        pltpu.VMEM((2, arows, DH), f32),
        pltpu.VMEM((2, 16, DH), f32),
        pltpu.VMEM((wrows, vrows), f32),
        pltpu.VMEM((DH, DH), f32),
        dma((4, n)), dma((4, n)),
        dma((2 * REACH,)), dma((2 * REACH,)),
        dma((n,)), dma((n,)),
        dma((3, n)), dma((3, n)),
    ]
    return pl.pallas_call(
        functools.partial(kernel, along, count),
        out_shape=[video, audio, video, video, video, audio, audio, audio],
        in_specs=[vmem] * 9 + [pl.BlockSpec(memory_space=pltpu.SMEM)],
        out_specs=[vmem] * 8,
        scratch_shapes=scratch,
        compiler_params=pltpu.CompilerParams(
            collective_id=0, has_side_effects=True, vmem_limit_bytes=40 * 1024 * 1024
        ),
        name="linked_attention",
    )(*args)


def solution(mesh):
    along = mesh.shape["audio"]
    count = mesh.shape["video"] * along
    rows = P(("clips", "video", "audio"), None)
    return jax.shard_map(
        functools.partial(on_device, along, count),
        mesh=mesh,
        in_specs=(rows,) * 6 + (P(),) + (rows,) * 3,
        out_specs=(rows,) * 8,
        check_vma=False,
    )
```

```python
import functools
import math

import jax
import jax.numpy as jnp
from jax import lax
from jax.experimental import pallas as pl
from jax.experimental.pallas import tpu as pltpu
from jax.sharding import PartitionSpec as P

DH = 128
FRAME = 960
AFRAME = 96
R = 2
SPAN = 5
EPSILON = 1e-06
HUGE = 1e30
SCALE = DH ** (-0.5)
SLOTS = (0, 1, 3, 4)
REACH = 2 * R
AUDIO_Q, AUDIO_DOUT, AUDIO_K, AUDIO_V = range(4)
D_KEY, D_VALUE, D_QUERY = range(3)
f32 = jnp.float32
bf16 = jnp.bfloat16


def nt(a, b):
    return lax.dot_general(a, b, (((1,), (1,)), ((), ())), preferred_element_type=f32)


def nn(a, b):
    return lax.dot_general(a, b, (((1,), (0,)), ((), ())), preferred_element_type=f32)


def tn(a, b):
    return lax.dot_general(a, b, (((0,), (0,)), ((), ())), preferred_element_type=f32)


def swapped(x):
    return pltpu.roll(x, DH // 2, 1)


def rinv_of(x):
    return lax.rsqrt(jnp.mean(x * x, axis=-1, keepdims=True) + EPSILON)


def turn(x, rinv, gain, cosine, sine):
    n = x * rinv * gain
    return n * cosine + swapped(n) * sine


def turn_back(dy, x, rinv, gain, cosine, sine):
    dn = dy * cosine - swapped(dy) * sine
    hat = x * rinv
    dh = dn * gain
    return rinv * (dh - hat * jnp.mean(dh * hat, axis=-1, keepdims=True))


def tables(places):
    lane = lax.broadcasted_iota(jnp.int32, places.shape, 1)
    half = DH // 2
    channel = jnp.where(lane < half, lane, lane - half).astype(f32)
    angles = places * jnp.exp(channel * (-2.0 * math.log(10000.0) / DH))
    sine = jnp.sin(angles)
    return jnp.cos(angles), jnp.where(lane < half, -sine, sine)


def kernel(
    along, count, h_vq, h_vk, h_vv, h_aq, h_ak, h_av, h_gain, h_vdo, h_ado, h_link,
    o_v, o_a, g_vq, g_vk, g_vv, g_aq, g_ak, g_av,
    win, po, po_in, gr, gr_in, stat, qv, kv, ea, dpa, pab, gab, rq, rk, tab_v, tab_a, coef, bias, wts,
    vq, vk, vv, aq, ak, gain, vdo, link, s_in,
    s_win, r_win, s_stat, r_stat, s_po, r_po, s_gr, r_gr,
):
    vrows, hd = vq.shape
    arows = aq.shape[0]
    heads = hd // DH
    wrows = SPAN * arows
    own = pl.ds(R * arows, arows)
    loads = [
        pltpu.make_async_copy(src, dst, s_in.at[i])
        for i, (src, dst) in enumerate(
            (
                (h_aq, aq), (h_ak, ak), (h_gain, gain),
                (h_ado, win.at[AUDIO_DOUT, own]), (h_av, win.at[AUDIO_V, own]),
                (h_vk, vk), (h_vq, vq), (h_vv, vv), (h_vdo, vdo), (h_link, link),
            )
        )
    ]
    for load in loads:
        load.start()
    clip = lax.axis_index("clips")
    me = lax.axis_index("video") * along + lax.axis_index("audio")

    def valid(i):
        return jnp.logical_and(i >= 0, i < count)

    def device(i):
        return (clip, i // along, lax.rem(i, along))

    def rows(j):
        return pl.ds(j * arows, arows)

    def lanes(h):
        return pl.ds(pl.multiple_of(h * DH, DH), DH)

    others = [d for d in range(-REACH, REACH + 1) if d]

    barrier = pltpu.get_barrier_semaphore()
    for d in others:

        @pl.when(valid(me + d))
        def _():
            pl.semaphore_signal(
                barrier, inc=1, device_id=device(me + d), device_id_type=pl.DeviceIdType.MESH
            )

    row = lax.broadcasted_iota(jnp.int32, (arows, DH), 0)
    c, s = tables((me * arows + row).astype(f32) / AFRAME)
    tab_a[0], tab_a[1] = c, s
    vplace = jnp.zeros((8, DH), jnp.int32) + (me * vrows) // FRAME
    c, s = tables(vplace.astype(f32))
    tab_v[0], tab_v[1] = c, s

    for load in loads[:3]:
        load.wait()

    def audio_prepare(h, _):
        hs = lanes(h)
        for src, slot, g in ((aq, AUDIO_Q, 2), (ak, AUDIO_K, 3)):
            x = src[:, hs].astype(f32)
            y = turn(x, rinv_of(x), gain[g : g + 1, hs], tab_a[0], tab_a[1])
            win[slot, rows(R), hs] = y.astype(bf16)
        return 0

    lax.fori_loop(0, heads, audio_prepare, 0, unroll=4)
    for load in loads[3:5]:
        load.wait()

    pl.semaphore_wait(barrier, jnp.minimum(me, REACH) + jnp.minimum(count - 1 - me, REACH))

    def win_copy(member, n, to):
        j = SLOTS[n]
        return pltpu.make_async_remote_copy(
            src_ref=win.at[member, rows(R)],
            dst_ref=win.at[member, rows(j)],
            send_sem=s_win.at[member, n],
            recv_sem=r_win.at[member, n],
            device_id=device(to),
            device_id_type=pl.DeviceIdType.MESH,
        )

    def back_copy(src, dst, send, recv, n, to):
        j = SLOTS[n]
        return pltpu.make_async_remote_copy(
            src_ref=src.at[rows(j)],
            dst_ref=dst.at[rows(j)],
            send_sem=send.at[n],
            recv_sem=recv.at[n],
            device_id=device(to),
            device_id_type=pl.DeviceIdType.MESH,
        )

    def stat_copy(d, to):
        n = others.index(d)
        return pltpu.make_async_remote_copy(
            src_ref=stat.at[REACH],
            dst_ref=stat.at[REACH - d],
            send_sem=s_stat.at[n],
            recv_sem=r_stat.at[n],
            device_id=device(to),
            device_id_type=pl.DeviceIdType.MESH,
        )

    def win_each(members, action):
        for member in members:
            for n, j in enumerate(SLOTS):
                other = me + j - R if action == "wait_recv" else me + R - j

                @pl.when(valid(other))
                def _():
                    getattr(win_copy(member, n, other), action)()

    def back_each(src, dst, send, recv, action):
        for n, j in enumerate(SLOTS):
            other = me + R - j if action == "wait_recv" else me + j - R

            @pl.when(valid(other))
            def _():
                getattr(back_copy(src, dst, send, recv, n, other), action)()

    def stat_each(action):
        for d in others:
            other = me - d if action == "wait_recv" else me + d

            @pl.when(valid(other))
            def _():
                getattr(stat_copy(d, other), action)()

    win_each((AUDIO_Q, AUDIO_DOUT, AUDIO_K, AUDIO_V), "start")

    for j in SLOTS:

        @pl.when(jnp.logical_not(valid(me + j - R)))
        def _():
            for member in range(4):
                win[member, rows(j), :] = jnp.zeros((arows, hd), bf16)

        @pl.when(jnp.logical_not(valid(me + R - j)))
        def _():
            po_in[rows(j), :] = jnp.zeros((arows, hd), bf16)
            for member in range(3):
                gr_in[member, rows(j), :] = jnp.zeros((arows, hd), bf16)

    empty = jnp.where(lax.broadcasted_iota(jnp.int32, (48, DH), 0) < 16, -HUGE, 0.0)
    stat[REACH] = empty
    for d in others:

        @pl.when(jnp.logical_not(valid(me - d)))
        def _():
            stat[REACH - d] = empty

    for load in loads[5:]:
        load.wait()
    lane_slot = lax.broadcasted_iota(jnp.int32, (1, wrows), 1) // arows
    linked_row = jnp.zeros((1, wrows), jnp.int32)
    for j in range(SPAN):
        on = link[0, j]
        bias[rows(j), :] = jnp.zeros((arows, vrows), f32) + jnp.where(on > 0, 0.0, -HUGE)
        linked_row = jnp.where(lane_slot == j, on, linked_row)
    linked_row = linked_row > 0

    def video_prepare(h, _):
        hs = lanes(h)
        for src, dst, keep, g in ((vq, qv, rq, 0), (vk, kv, rk, 1)):
            x = src[:, hs].astype(f32)
            rinv = rinv_of(x)
            keep[:, hs] = jnp.broadcast_to(rinv, (vrows, DH))
            y = turn(x, rinv, gain[g : g + 1, hs], tab_v[0, 0:1], tab_v[1, 0:1])
            dst[:, hs] = y.astype(bf16)
        return 0

    lax.fori_loop(0, heads, video_prepare, 0, unroll=4)

    win_each((AUDIO_Q, AUDIO_DOUT), "wait_recv")

    def audio_forward(h, _):
        hs = lanes(h)
        v = vv[:, hs]
        r = nt(kv[:, hs], win[AUDIO_Q, :, hs]) * SCALE
        top = jnp.max(r, axis=0, keepdims=True)
        e = jnp.exp(r - top)
        ea[h] = e
        dp = nt(v, win[AUDIO_DOUT, :, hs])
        dpa[h] = dp
        stat[REACH, pl.ds(h, 1), 0:wrows] = jnp.where(linked_row, top, -HUGE)
        stat[REACH, pl.ds(16 + h, 1), 0:wrows] = jnp.where(
            linked_row, jnp.sum(e, axis=0, keepdims=True), 0.0
        )
        stat[REACH, pl.ds(32 + h, 1), 0:wrows] = jnp.where(
            linked_row, jnp.sum(e * dp, axis=0, keepdims=True), 0.0
        )
        po[:, hs] = tn(e.astype(bf16), v).astype(bf16)
        return 0

    lax.fori_loop(0, heads, audio_forward, 0, unroll=4)
    stat_each("start")
    back_each(po, po_in, s_po, r_po, "start")

    win_each((AUDIO_K, AUDIO_V), "wait_recv")

    def video_side(h, _):
        hs = lanes(h)
        ka, va = win[AUDIO_K, :, hs], win[AUDIO_V, :, hs]
        q, do = qv[:, hs], vdo[:, hs]
        sc = nt(ka, q) * SCALE + bias[...]
        top = jnp.max(sc, axis=0, keepdims=True)
        e = jnp.exp(sc - top)
        p = e * (1.0 / jnp.sum(e, axis=0, keepdims=True))
        pb = p.astype(bf16)
        o_v[:, hs] = tn(pb, va).astype(bf16)
        dp = nt(va, do)
        delta = jnp.sum(p * dp, axis=0, keepdims=True)
        gs = (p * (dp - delta)).astype(bf16)
        gr[D_KEY, :, hs] = (nn(gs, q) * SCALE).astype(bf16)
        gr[D_VALUE, :, hs] = nn(pb, do).astype(bf16)
        dq = tn(gs, ka) * SCALE
        g_vq[:, hs] = turn_back(
            dq, vq[:, hs].astype(f32), rq[:, hs], gain[0:1, hs], tab_v[0, 0:1], tab_v[1, 0:1]
        ).astype(bf16)
        return 0

    lax.fori_loop(0, heads, video_side, 0, unroll=4)
    for member in (D_KEY, D_VALUE):
        back_each(gr.at[member], gr_in.at[member], s_gr.at[member], r_gr.at[member], "start")

    stat_each("wait_recv")
    lane = lax.broadcasted_iota(jnp.int32, (16, DH), 1)
    tops, totals, dots = [], [], []
    for t in range(2 * REACH + 1):
        shift = (t - REACH) * arows
        inside = jnp.logical_and(lane >= shift, lane < shift + wrows)
        rolled = [
            pltpu.roll(stat[t, 16 * i : 16 * i + 16], shift % DH, 1) if shift else stat[t, 16 * i : 16 * i + 16]
            for i in range(3)
        ]
        tops.append(jnp.where(inside, rolled[0], -HUGE))
        totals.append(jnp.where(inside, rolled[1], 0.0))
        dots.append(jnp.where(inside, rolled[2], 0.0))
    best = functools.reduce(jnp.maximum, tops)
    factors = [jnp.where(a > -0.5 * HUGE, jnp.exp(a - best), 0.0) for a in tops]
    total = sum(a * b for a, b in zip(factors, totals))
    inverse = 1.0 / jnp.where(total > 0.0, total, 1.0)
    coef[0] = factors[REACH] * inverse
    coef[1] = sum(a * b for a, b in zip(factors, dots)) * inverse
    wts[...] = jnp.zeros(wts.shape, f32)
    for j in range(SPAN):
        wts[16 * j : 16 * j + 16, :] = factors[REACH + R - j] * inverse

    def audio_back(h, _):
        hs = lanes(h)
        p = ea[h] * coef[0, pl.ds(h, 1), 0:wrows]
        ga = (p * (dpa[h] - coef[1, pl.ds(h, 1), 0:wrows])).astype(bf16)
        pab[h] = p.astype(bf16)
        gab[h] = ga
        gr[D_QUERY, :, hs] = (tn(ga, kv[:, hs]) * SCALE).astype(bf16)
        return 0

    lax.fori_loop(0, heads, audio_back, 0, unroll=4)
    back_each(gr.at[D_QUERY], gr_in.at[D_QUERY], s_gr.at[D_QUERY], r_gr.at[D_QUERY], "start")

    def video_back(h, _):
        hs = lanes(h)
        g_vv[:, hs] = nn(pab[h], win[AUDIO_DOUT, :, hs]).astype(bf16)
        dk = nn(gab[h], win[AUDIO_Q, :, hs]) * SCALE
        g_vk[:, hs] = turn_back(
            dk, vk[:, hs].astype(f32), rk[:, hs], gain[1:2, hs], tab_v[0, 0:1], tab_v[1, 0:1]
        ).astype(bf16)
        return 0

    lax.fori_loop(0, heads, video_back, 0, unroll=4)

    turned = jnp.transpose(wts[...])[R * arows : (R + 1) * arows, :]
    back_each(po, po_in, s_po, r_po, "wait_recv")
    for h in range(heads):
        hs = slice(h * DH, (h + 1) * DH)
        acc = jnp.zeros((arows, DH), f32)
        for j in range(SPAN):
            part = (po if j == R else po_in)[j * arows : (j + 1) * arows, hs].astype(f32)
            acc += turned[:, 16 * j + h : 16 * j + h + 1] * part
        o_a[:, hs] = acc.astype(bf16)

    def merged(member, hs):
        acc = gr[member, rows(R), hs].astype(f32)
        for j in SLOTS:
            acc += gr_in[member, rows(j), hs].astype(f32)
        return acc

    def audio_grad(src, member, g, dst):
        def body(h, _):
            hs = lanes(h)
            x = src[:, hs].astype(f32)
            dst[:, hs] = turn_back(
                merged(member, hs), x, rinv_of(x), gain[g : g + 1, hs], tab_a[0], tab_a[1]
            ).astype(bf16)
            return 0

        lax.fori_loop(0, heads, body, 0, unroll=4)

    for member in (D_KEY, D_VALUE):
        back_each(gr.at[member], gr_in.at[member], s_gr.at[member], r_gr.at[member], "wait_recv")
    g_av[...] = merged(D_VALUE, slice(None)).astype(bf16)
    audio_grad(ak, D_KEY, 3, g_ak)
    back_each(gr.at[D_QUERY], gr_in.at[D_QUERY], s_gr.at[D_QUERY], r_gr.at[D_QUERY], "wait_recv")
    audio_grad(aq, D_QUERY, 2, g_aq)

    win_each(range(4), "wait_send")
    stat_each("wait_send")
    back_each(po, po_in, s_po, r_po, "wait_send")
    for member in range(3):
        back_each(gr.at[member], gr_in.at[member], s_gr.at[member], r_gr.at[member], "wait_send")


def write_out(*refs):
    n = len(refs) // 2
    sems = refs[-1]
    copies = [pltpu.make_async_copy(refs[i], refs[n + i], sems.at[i]) for i in range(n)]
    for copy in copies:
        copy.start()
    for copy in copies:
        copy.wait()


def on_device(along, count, *args):
    vq, aq = args[0], args[3]
    vrows, hd = vq.shape
    arows = aq.shape[0]
    heads = hd // DH
    wrows = SPAN * arows
    video = jax.ShapeDtypeStruct((vrows, hd), bf16)
    audio = jax.ShapeDtypeStruct((arows, hd), bf16)
    vmem = pl.BlockSpec(memory_space=pltpu.VMEM)
    dma = pltpu.SemaphoreType.DMA
    n = len(SLOTS)
    scratch = [
        pltpu.VMEM((4, wrows, hd), bf16),
        pltpu.VMEM((wrows, hd), bf16),
        pltpu.VMEM((wrows, hd), bf16),
        pltpu.VMEM((3, wrows, hd), bf16),
        pltpu.VMEM((3, wrows, hd), bf16),
        pltpu.VMEM((2 * REACH + 1, 48, DH), f32),
        pltpu.VMEM((vrows, hd), bf16),
        pltpu.VMEM((vrows, hd), bf16),
        pltpu.VMEM((heads, vrows, wrows), f32),
        pltpu.VMEM((heads, vrows, wrows), f32),
        pltpu.VMEM((heads, vrows, wrows), bf16),
        pltpu.VMEM((heads, vrows, wrows), bf16),
        pltpu.VMEM((vrows, hd), f32),
        pltpu.VMEM((vrows, hd), f32),
        pltpu.VMEM((2, 8, DH), f32),
        pltpu.VMEM((2, arows, DH), f32),
        pltpu.VMEM((2, 16, DH), f32),
        pltpu.VMEM((wrows, vrows), f32),
        pltpu.VMEM((DH, DH), f32),
        pltpu.VMEM((vrows, hd), bf16),
        pltpu.VMEM((vrows, hd), bf16),
        pltpu.VMEM((vrows, hd), bf16),
        pltpu.VMEM((arows, hd), bf16),
        pltpu.VMEM((arows, hd), bf16),
        pltpu.VMEM(args[6].shape, f32),
        pltpu.VMEM((vrows, hd), bf16),
        pltpu.SMEM(args[9].shape, jnp.int32),
        dma((10,)),
        dma((4, n)), dma((4, n)),
        dma((2 * REACH,)), dma((2 * REACH,)),
        dma((n,)), dma((n,)),
        dma((3, n)), dma((3, n)),
    ]
    results = pl.pallas_call(
        functools.partial(kernel, along, count),
        out_shape=[video, audio, video, video, video, audio, audio, audio],
        in_specs=[pl.BlockSpec(memory_space=pl.ANY)] * 10,
        out_specs=[vmem] * 8,
        scratch_shapes=scratch,
        compiler_params=pltpu.CompilerParams(
            collective_id=0, has_side_effects=True, vmem_limit_bytes=56 * 1024 * 1024
        ),
        name="linked_attention",
    )(*args)
    return pl.pallas_call(
        write_out,
        out_shape=[video, audio, video, video, video, audio, audio, audio],
        in_specs=[vmem] * 8,
        out_specs=[pl.BlockSpec(memory_space=pl.ANY)] * 8,
        scratch_shapes=[dma((8,))],
        name="write_out",
    )(*results)


def solution(mesh):
    along = mesh.shape["audio"]
    count = mesh.shape["video"] * along
    rows = P(("clips", "video", "audio"), None)
    return jax.shard_map(
        functools.partial(on_device, along, count),
        mesh=mesh,
        in_specs=(rows,) * 6 + (P(),) + (rows,) * 3,
        out_specs=(rows,) * 8,
        check_vma=False,
    )
```

```python
import functools
import math

import jax
import jax.numpy as jnp
from jax import lax
from jax.experimental import pallas as pl
from jax.experimental.pallas import tpu as pltpu
from jax.sharding import PartitionSpec as P

DH = 128
FRAME = 960
AFRAME = 96
R = 2
SPAN = 5
EPSILON = 1e-06
HUGE = 1e30
SCALE = DH ** (-0.5)
SLOTS = (0, 1, 3, 4)
REACH = 2 * R
AUDIO_Q, AUDIO_DOUT, AUDIO_K, AUDIO_V = range(4)
D_KEY, D_VALUE, D_QUERY = range(3)
f32 = jnp.float32
bf16 = jnp.bfloat16


def nt(a, b):
    return lax.dot_general(a, b, (((1,), (1,)), ((), ())), preferred_element_type=f32)


def nn(a, b):
    return lax.dot_general(a, b, (((1,), (0,)), ((), ())), preferred_element_type=f32)


def tn(a, b):
    return lax.dot_general(a, b, (((0,), (0,)), ((), ())), preferred_element_type=f32)


def swapped(x):
    return pltpu.roll(x, DH // 2, 1)


def rinv_of(x):
    return lax.rsqrt(jnp.mean(x * x, axis=-1, keepdims=True) + EPSILON)


def turn(x, rinv, gain, cosine, sine):
    n = x * rinv * gain
    return n * cosine + swapped(n) * sine


def turn_back(dy, x, rinv, gain, cosine, sine):
    dn = dy * cosine - swapped(dy) * sine
    hat = x * rinv
    dh = dn * gain
    return rinv * (dh - hat * jnp.mean(dh * hat, axis=-1, keepdims=True))


def tables(places):
    lane = lax.broadcasted_iota(jnp.int32, places.shape, 1)
    half = DH // 2
    channel = jnp.where(lane < half, lane, lane - half).astype(f32)
    angles = places * jnp.exp(channel * (-2.0 * math.log(10000.0) / DH))
    sine = jnp.sin(angles)
    return jnp.cos(angles), jnp.where(lane < half, -sine, sine)


def kernel(
    along, count, h_vq, h_vk, h_vv, h_aq, h_ak, h_av, h_gain, h_vdo, h_ado, h_link,
    o_v, o_a, g_vq, g_vk, g_vv, g_aq, g_ak, g_av,
    win, po, po_in, gr, gr_in, stat, qv, kv, ea, dpa, pab, gab, rq, rk, tab_v, tab_a, coef, bias, wts,
    vq, vk, vv, aq, ak, gain, vdo, link, s_in,
    s_win, r_win, s_stat, r_stat, s_po, r_po, s_gr, r_gr,
):
    vrows, hd = vq.shape
    arows = aq.shape[0]
    heads = hd // DH
    wrows = SPAN * arows
    own = pl.ds(R * arows, arows)
    loads = [
        pltpu.make_async_copy(src, dst, s_in.at[i])
        for i, (src, dst) in enumerate(
            (
                (h_aq, aq), (h_ak, ak), (h_gain, gain),
                (h_ado, win.at[AUDIO_DOUT, own]), (h_av, win.at[AUDIO_V, own]),
                (h_vk, vk), (h_vq, vq), (h_vv, vv), (h_vdo, vdo), (h_link, link),
            )
        )
    ]
    for load in loads:
        load.start()
    clip = lax.axis_index("clips")
    me = lax.axis_index("video") * along + lax.axis_index("audio")

    def valid(i):
        return jnp.logical_and(i >= 0, i < count)

    def device(i):
        return (clip, i // along, lax.rem(i, along))

    def rows(j):
        return pl.ds(j * arows, arows)

    def lanes(h):
        return pl.ds(pl.multiple_of(h * DH, DH), DH)

    others = [d for d in range(-REACH, REACH + 1) if d]

    barrier = pltpu.get_barrier_semaphore()
    for d in others:

        @pl.when(valid(me + d))
        def _():
            pl.semaphore_signal(
                barrier, inc=1, device_id=device(me + d), device_id_type=pl.DeviceIdType.MESH
            )

    row = lax.broadcasted_iota(jnp.int32, (arows, DH), 0)
    c, s = tables((me * arows + row).astype(f32) / AFRAME)
    tab_a[0], tab_a[1] = c, s
    vplace = jnp.zeros((8, DH), jnp.int32) + (me * vrows) // FRAME
    c, s = tables(vplace.astype(f32))
    tab_v[0], tab_v[1] = c, s

    for load in loads[:3]:
        load.wait()

    def audio_prepare(h, _):
        hs = lanes(h)
        for src, slot, g in ((aq, AUDIO_Q, 2), (ak, AUDIO_K, 3)):
            x = src[:, hs].astype(f32)
            y = turn(x, rinv_of(x), gain[g : g + 1, hs], tab_a[0], tab_a[1])
            win[slot, rows(R), hs] = y.astype(bf16)
        return 0

    lax.fori_loop(0, heads, audio_prepare, 0, unroll=4)
    for load in loads[3:5]:
        load.wait()

    pl.semaphore_wait(barrier, jnp.minimum(me, REACH) + jnp.minimum(count - 1 - me, REACH))

    def win_copy(member, n, to):
        j = SLOTS[n]
        return pltpu.make_async_remote_copy(
            src_ref=win.at[member, rows(R)],
            dst_ref=win.at[member, rows(j)],
            send_sem=s_win.at[member, n],
            recv_sem=r_win.at[member, n],
            device_id=device(to),
            device_id_type=pl.DeviceIdType.MESH,
        )

    def back_copy(src, dst, send, recv, n, to):
        j = SLOTS[n]
        return pltpu.make_async_remote_copy(
            src_ref=src.at[rows(j)],
            dst_ref=dst.at[rows(j)],
            send_sem=send.at[n],
            recv_sem=recv.at[n],
            device_id=device(to),
            device_id_type=pl.DeviceIdType.MESH,
        )

    def stat_copy(d, to):
        n = others.index(d)
        return pltpu.make_async_remote_copy(
            src_ref=stat.at[REACH],
            dst_ref=stat.at[REACH - d],
            send_sem=s_stat.at[n],
            recv_sem=r_stat.at[n],
            device_id=device(to),
            device_id_type=pl.DeviceIdType.MESH,
        )

    even = lax.rem(me, 2) == 0

    def win_each(members, action, slots=range(len(SLOTS))):
        for member in members:
            for n in slots:
                j = SLOTS[n]
                other = me + j - R if action == "wait_recv" else me + R - j
                go = valid(other)
                if action != "wait_recv" and j == 0:
                    go = jnp.logical_and(go, even)
                if action != "wait_recv" and j == SPAN - 1:
                    go = jnp.logical_and(go, jnp.logical_not(even))

                @pl.when(go)
                def _():
                    getattr(win_copy(member, n, other), action)()

    def pass_on(members, action):
        for member in members:
            for parity, near, n, spare, step in ((0, 1, 0, 3, 1), (1, 3, 3, 0, -1)):
                go = jnp.logical_and(valid(me - step), valid(me + step))

                @pl.when(jnp.logical_and(go, lax.rem(me, 2) == parity))
                def _():
                    copy = pltpu.make_async_remote_copy(
                        src_ref=win.at[member, rows(near)],
                        dst_ref=win.at[member, rows(SLOTS[n])],
                        send_sem=s_win.at[member, spare],
                        recv_sem=r_win.at[member, n],
                        device_id=device(me + step),
                        device_id_type=pl.DeviceIdType.MESH,
                    )
                    getattr(copy, action)()

    def win_arrive(members):
        win_each(members, "wait_recv", (1, 2))
        pass_on(members, "start")
        win_each(members, "wait_recv", (0, 3))

    def back_each(src, dst, send, recv, action):
        for n, j in enumerate(SLOTS):
            other = me + R - j if action == "wait_recv" else me + j - R

            @pl.when(valid(other))
            def _():
                getattr(back_copy(src, dst, send, recv, n, other), action)()

    def stat_each(action):
        for d in others:
            other = me - d if action == "wait_recv" else me + d

            @pl.when(valid(other))
            def _():
                getattr(stat_copy(d, other), action)()

    win_each((AUDIO_Q, AUDIO_DOUT, AUDIO_K, AUDIO_V), "start")

    for j in SLOTS:

        @pl.when(jnp.logical_not(valid(me + j - R)))
        def _():
            for member in range(4):
                win[member, rows(j), :] = jnp.zeros((arows, hd), bf16)

        @pl.when(jnp.logical_not(valid(me + R - j)))
        def _():
            po_in[rows(j), :] = jnp.zeros((arows, hd), bf16)
            for member in range(3):
                gr_in[member, rows(j), :] = jnp.zeros((arows, hd), bf16)

    empty = jnp.where(lax.broadcasted_iota(jnp.int32, (48, DH), 0) < 16, -HUGE, 0.0)
    stat[REACH] = empty
    for d in others:

        @pl.when(jnp.logical_not(valid(me - d)))
        def _():
            stat[REACH - d] = empty

    for load in loads[5:]:
        load.wait()
    lane_slot = lax.broadcasted_iota(jnp.int32, (1, wrows), 1) // arows
    linked_row = jnp.zeros((1, wrows), jnp.int32)
    for j in range(SPAN):
        on = link[0, j]
        bias[rows(j), :] = jnp.zeros((arows, vrows), f32) + jnp.where(on > 0, 0.0, -HUGE)
        linked_row = jnp.where(lane_slot == j, on, linked_row)
    linked_row = linked_row > 0

    def video_prepare(h, _):
        hs = lanes(h)
        for src, dst, keep, g in ((vq, qv, rq, 0), (vk, kv, rk, 1)):
            x = src[:, hs].astype(f32)
            rinv = rinv_of(x)
            keep[:, hs] = jnp.broadcast_to(rinv, (vrows, DH))
            y = turn(x, rinv, gain[g : g + 1, hs], tab_v[0, 0:1], tab_v[1, 0:1])
            dst[:, hs] = y.astype(bf16)
        return 0

    lax.fori_loop(0, heads, video_prepare, 0, unroll=4)

    win_arrive((AUDIO_Q, AUDIO_DOUT))

    def audio_forward(h, _):
        hs = lanes(h)
        v = vv[:, hs]
        r = nt(kv[:, hs], win[AUDIO_Q, :, hs]) * SCALE
        top = jnp.max(r, axis=0, keepdims=True)
        e = jnp.exp(r - top)
        ea[h] = e
        dp = nt(v, win[AUDIO_DOUT, :, hs])
        dpa[h] = dp
        stat[REACH, pl.ds(h, 1), 0:wrows] = jnp.where(linked_row, top, -HUGE)
        stat[REACH, pl.ds(16 + h, 1), 0:wrows] = jnp.where(
            linked_row, jnp.sum(e, axis=0, keepdims=True), 0.0
        )
        stat[REACH, pl.ds(32 + h, 1), 0:wrows] = jnp.where(
            linked_row, jnp.sum(e * dp, axis=0, keepdims=True), 0.0
        )
        po[:, hs] = tn(e.astype(bf16), v).astype(bf16)
        return 0

    lax.fori_loop(0, heads, audio_forward, 0, unroll=4)
    stat_each("start")
    back_each(po, po_in, s_po, r_po, "start")

    win_arrive((AUDIO_K, AUDIO_V))

    def video_side(h, _):
        hs = lanes(h)
        ka, va = win[AUDIO_K, :, hs], win[AUDIO_V, :, hs]
        q, do = qv[:, hs], vdo[:, hs]
        sc = nt(ka, q) * SCALE + bias[...]
        top = jnp.max(sc, axis=0, keepdims=True)
        e = jnp.exp(sc - top)
        p = e * (1.0 / jnp.sum(e, axis=0, keepdims=True))
        pb = p.astype(bf16)
        o_v[:, hs] = tn(pb, va).astype(bf16)
        dp = nt(va, do)
        delta = jnp.sum(p * dp, axis=0, keepdims=True)
        gs = (p * (dp - delta)).astype(bf16)
        gr[D_KEY, :, hs] = (nn(gs, q) * SCALE).astype(bf16)
        gr[D_VALUE, :, hs] = nn(pb, do).astype(bf16)
        dq = tn(gs, ka) * SCALE
        g_vq[:, hs] = turn_back(
            dq, vq[:, hs].astype(f32), rq[:, hs], gain[0:1, hs], tab_v[0, 0:1], tab_v[1, 0:1]
        ).astype(bf16)
        return 0

    lax.fori_loop(0, heads, video_side, 0, unroll=4)
    for member in (D_KEY, D_VALUE):
        back_each(gr.at[member], gr_in.at[member], s_gr.at[member], r_gr.at[member], "start")

    stat_each("wait_recv")
    lane = lax.broadcasted_iota(jnp.int32, (16, DH), 1)
    tops, totals, dots = [], [], []
    for t in range(2 * REACH + 1):
        shift = (t - REACH) * arows
        inside = jnp.logical_and(lane >= shift, lane < shift + wrows)
        rolled = [
            pltpu.roll(stat[t, 16 * i : 16 * i + 16], shift % DH, 1) if shift else stat[t, 16 * i : 16 * i + 16]
            for i in range(3)
        ]
        tops.append(jnp.where(inside, rolled[0], -HUGE))
        totals.append(jnp.where(inside, rolled[1], 0.0))
        dots.append(jnp.where(inside, rolled[2], 0.0))
    best = functools.reduce(jnp.maximum, tops)
    factors = [jnp.where(a > -0.5 * HUGE, jnp.exp(a - best), 0.0) for a in tops]
    total = sum(a * b for a, b in zip(factors, totals))
    inverse = 1.0 / jnp.where(total > 0.0, total, 1.0)
    coef[0] = factors[REACH] * inverse
    coef[1] = sum(a * b for a, b in zip(factors, dots)) * inverse
    wts[...] = jnp.zeros(wts.shape, f32)
    for j in range(SPAN):
        wts[16 * j : 16 * j + 16, :] = factors[REACH + R - j] * inverse

    def audio_back(h, _):
        hs = lanes(h)
        p = ea[h] * coef[0, pl.ds(h, 1), 0:wrows]
        ga = (p * (dpa[h] - coef[1, pl.ds(h, 1), 0:wrows])).astype(bf16)
        pab[h] = p.astype(bf16)
        gab[h] = ga
        gr[D_QUERY, :, hs] = (tn(ga, kv[:, hs]) * SCALE).astype(bf16)
        return 0

    lax.fori_loop(0, heads, audio_back, 0, unroll=4)
    back_each(gr.at[D_QUERY], gr_in.at[D_QUERY], s_gr.at[D_QUERY], r_gr.at[D_QUERY], "start")

    def video_back(h, _):
        hs = lanes(h)
        g_vv[:, hs] = nn(pab[h], win[AUDIO_DOUT, :, hs]).astype(bf16)
        dk = nn(gab[h], win[AUDIO_Q, :, hs]) * SCALE
        g_vk[:, hs] = turn_back(
            dk, vk[:, hs].astype(f32), rk[:, hs], gain[1:2, hs], tab_v[0, 0:1], tab_v[1, 0:1]
        ).astype(bf16)
        return 0

    lax.fori_loop(0, heads, video_back, 0, unroll=4)

    turned = jnp.transpose(wts[...])[R * arows : (R + 1) * arows, :]
    back_each(po, po_in, s_po, r_po, "wait_recv")
    for h in range(heads):
        hs = slice(h * DH, (h + 1) * DH)
        acc = jnp.zeros((arows, DH), f32)
        for j in range(SPAN):
            part = (po if j == R else po_in)[j * arows : (j + 1) * arows, hs].astype(f32)
            acc += turned[:, 16 * j + h : 16 * j + h + 1] * part
        o_a[:, hs] = acc.astype(bf16)

    def merged(member, hs):
        acc = gr[member, rows(R), hs].astype(f32)
        for j in SLOTS:
            acc += gr_in[member, rows(j), hs].astype(f32)
        return acc

    def audio_grad(src, member, g, dst):
        def body(h, _):
            hs = lanes(h)
            x = src[:, hs].astype(f32)
            dst[:, hs] = turn_back(
                merged(member, hs), x, rinv_of(x), gain[g : g + 1, hs], tab_a[0], tab_a[1]
            ).astype(bf16)
            return 0

        lax.fori_loop(0, heads, body, 0, unroll=4)

    for member in (D_KEY, D_VALUE):
        back_each(gr.at[member], gr_in.at[member], s_gr.at[member], r_gr.at[member], "wait_recv")
    g_av[...] = merged(D_VALUE, slice(None)).astype(bf16)
    audio_grad(ak, D_KEY, 3, g_ak)
    back_each(gr.at[D_QUERY], gr_in.at[D_QUERY], s_gr.at[D_QUERY], r_gr.at[D_QUERY], "wait_recv")
    audio_grad(aq, D_QUERY, 2, g_aq)

    win_each(range(4), "wait_send")
    pass_on(range(4), "wait_send")
    stat_each("wait_send")
    back_each(po, po_in, s_po, r_po, "wait_send")
    for member in range(3):
        back_each(gr.at[member], gr_in.at[member], s_gr.at[member], r_gr.at[member], "wait_send")


def write_out(*refs):
    n = len(refs) // 2
    sems = refs[-1]
    copies = [pltpu.make_async_copy(refs[i], refs[n + i], sems.at[i]) for i in range(n)]
    for copy in copies:
        copy.start()
    for copy in copies:
        copy.wait()


def on_device(along, count, *args):
    vq, aq = args[0], args[3]
    vrows, hd = vq.shape
    arows = aq.shape[0]
    heads = hd // DH
    wrows = SPAN * arows
    video = jax.ShapeDtypeStruct((vrows, hd), bf16)
    audio = jax.ShapeDtypeStruct((arows, hd), bf16)
    vmem = pl.BlockSpec(memory_space=pltpu.VMEM)
    dma = pltpu.SemaphoreType.DMA
    n = len(SLOTS)
    scratch = [
        pltpu.VMEM((4, wrows, hd), bf16),
        pltpu.VMEM((wrows, hd), bf16),
        pltpu.VMEM((wrows, hd), bf16),
        pltpu.VMEM((3, wrows, hd), bf16),
        pltpu.VMEM((3, wrows, hd), bf16),
        pltpu.VMEM((2 * REACH + 1, 48, DH), f32),
        pltpu.VMEM((vrows, hd), bf16),
        pltpu.VMEM((vrows, hd), bf16),
        pltpu.VMEM((heads, vrows, wrows), f32),
        pltpu.VMEM((heads, vrows, wrows), f32),
        pltpu.VMEM((heads, vrows, wrows), bf16),
        pltpu.VMEM((heads, vrows, wrows), bf16),
        pltpu.VMEM((vrows, hd), f32),
        pltpu.VMEM((vrows, hd), f32),
        pltpu.VMEM((2, 8, DH), f32),
        pltpu.VMEM((2, arows, DH), f32),
        pltpu.VMEM((2, 16, DH), f32),
        pltpu.VMEM((wrows, vrows), f32),
        pltpu.VMEM((DH, DH), f32),
        pltpu.VMEM((vrows, hd), bf16),
        pltpu.VMEM((vrows, hd), bf16),
        pltpu.VMEM((vrows, hd), bf16),
        pltpu.VMEM((arows, hd), bf16),
        pltpu.VMEM((arows, hd), bf16),
        pltpu.VMEM(args[6].shape, f32),
        pltpu.VMEM((vrows, hd), bf16),
        pltpu.SMEM(args[9].shape, jnp.int32),
        dma((10,)),
        dma((4, n)), dma((4, n)),
        dma((2 * REACH,)), dma((2 * REACH,)),
        dma((n,)), dma((n,)),
        dma((3, n)), dma((3, n)),
    ]
    results = pl.pallas_call(
        functools.partial(kernel, along, count),
        out_shape=[video, audio, video, video, video, audio, audio, audio],
        in_specs=[pl.BlockSpec(memory_space=pl.ANY)] * 10,
        out_specs=[vmem] * 8,
        scratch_shapes=scratch,
        compiler_params=pltpu.CompilerParams(
            collective_id=0, has_side_effects=True, vmem_limit_bytes=56 * 1024 * 1024
        ),
        name="linked_attention",
    )(*args)
    return pl.pallas_call(
        write_out,
        out_shape=[video, audio, video, video, video, audio, audio, audio],
        in_specs=[vmem] * 8,
        out_specs=[pl.BlockSpec(memory_space=pl.ANY)] * 8,
        scratch_shapes=[dma((8,))],
        name="write_out",
    )(*results)


def solution(mesh):
    along = mesh.shape["audio"]
    count = mesh.shape["video"] * along
    rows = P(("clips", "video", "audio"), None)
    return jax.shard_map(
        functools.partial(on_device, along, count),
        mesh=mesh,
        in_specs=(rows,) * 6 + (P(),) + (rows,) * 3,
        out_specs=(rows,) * 8,
        check_vma=False,
    )
```

```python
import functools
import math

import jax
import jax.numpy as jnp
from jax import lax
from jax.experimental import pallas as pl
from jax.experimental.pallas import tpu as pltpu
from jax.sharding import PartitionSpec as P

DH = 128
FRAME = 960
AFRAME = 96
R = 2
SPAN = 5
EPSILON = 1e-06
HUGE = 1e30
SCALE = DH ** (-0.5)
SLOTS = (0, 1, 3, 4)
REACH = 2 * R
AUDIO_Q, AUDIO_DOUT, AUDIO_K, AUDIO_V = range(4)
D_KEY, D_VALUE, D_QUERY = range(3)
f32 = jnp.float32
bf16 = jnp.bfloat16


def nt(a, b):
    return lax.dot_general(a, b, (((1,), (1,)), ((), ())), preferred_element_type=f32)


def nn(a, b):
    return lax.dot_general(a, b, (((1,), (0,)), ((), ())), preferred_element_type=f32)


def tn(a, b):
    return lax.dot_general(a, b, (((0,), (0,)), ((), ())), preferred_element_type=f32)


def swapped(x):
    return pltpu.roll(x, DH // 2, 1)


def rinv_of(x):
    return lax.rsqrt(jnp.mean(x * x, axis=-1, keepdims=True) + EPSILON)


def turn(x, rinv, gain, cosine, sine):
    n = x * rinv * gain
    return n * cosine + swapped(n) * sine


def turn_back(dy, x, rinv, gain, cosine, sine):
    dn = dy * cosine - swapped(dy) * sine
    hat = x * rinv
    dh = dn * gain
    return rinv * (dh - hat * jnp.mean(dh * hat, axis=-1, keepdims=True))


def tables(places):
    lane = lax.broadcasted_iota(jnp.int32, places.shape, 1)
    half = DH // 2
    channel = jnp.where(lane < half, lane, lane - half).astype(f32)
    angles = places * jnp.exp(channel * (-2.0 * math.log(10000.0) / DH))
    sine = jnp.sin(angles)
    return jnp.cos(angles), jnp.where(lane < half, -sine, sine)


def kernel(
    along, count, h_vq, h_vk, h_vv, h_aq, h_ak, h_av, h_gain, h_vdo, h_ado, h_link,
    o_v, o_a, g_vq, g_vk, g_vv, g_aq, g_ak, g_av,
    win, po, po_in, gr, gr_in, stat, qv, kv, ea, dpa, pab, gab, rq, rk, tab_v, tab_a, coef, bias, wts,
    vq, vk, vv, aq, ak, gain, vdo, link, s_in,
    s_win, r_win, s_stat, r_stat, s_po, r_po, s_gr, r_gr, hand, s_hand, r_hand,
):
    vrows, hd = vq.shape
    arows = aq.shape[0]
    heads = hd // DH
    wrows = SPAN * arows
    own = pl.ds(R * arows, arows)
    loads = [
        pltpu.make_async_copy(src, dst, s_in.at[i])
        for i, (src, dst) in enumerate(
            (
                (h_aq, aq), (h_ak, ak), (h_gain, gain),
                (h_ado, win.at[AUDIO_DOUT, own]), (h_av, win.at[AUDIO_V, own]),
                (h_vk, vk), (h_vq, vq), (h_vv, vv), (h_vdo, vdo), (h_link, link),
            )
        )
    ]
    for load in loads:
        load.start()
    clip = lax.axis_index("clips")
    me = lax.axis_index("video") * along + lax.axis_index("audio")

    def valid(i):
        return jnp.logical_and(i >= 0, i < count)

    def device(i):
        return (clip, i // along, lax.rem(i, along))

    def rows(j):
        return pl.ds(j * arows, arows)

    def lanes(h):
        return pl.ds(pl.multiple_of(h * DH, DH), DH)

    others = [d for d in range(-REACH, REACH + 1) if d]

    barrier = pltpu.get_barrier_semaphore()
    for d in others:

        @pl.when(valid(me + d))
        def _():
            pl.semaphore_signal(
                barrier, inc=1, device_id=device(me + d), device_id_type=pl.DeviceIdType.MESH
            )

    row = lax.broadcasted_iota(jnp.int32, (arows, DH), 0)
    c, s = tables((me * arows + row).astype(f32) / AFRAME)
    tab_a[0], tab_a[1] = c, s
    vplace = jnp.zeros((8, DH), jnp.int32) + (me * vrows) // FRAME
    c, s = tables(vplace.astype(f32))
    tab_v[0], tab_v[1] = c, s

    for load in loads[:3]:
        load.wait()

    def audio_prepare(h, _):
        hs = lanes(h)
        for src, slot, g in ((aq, AUDIO_Q, 2), (ak, AUDIO_K, 3)):
            x = src[:, hs].astype(f32)
            y = turn(x, rinv_of(x), gain[g : g + 1, hs], tab_a[0], tab_a[1])
            win[slot, rows(R), hs] = y.astype(bf16)
        return 0

    lax.fori_loop(0, heads, audio_prepare, 0, unroll=4)
    for load in loads[3:5]:
        load.wait()

    pl.semaphore_wait(barrier, jnp.minimum(me, REACH) + jnp.minimum(count - 1 - me, REACH))

    def win_copy(member, n, to):
        j = SLOTS[n]
        return pltpu.make_async_remote_copy(
            src_ref=win.at[member, rows(R)],
            dst_ref=win.at[member, rows(j)],
            send_sem=s_win.at[member, n],
            recv_sem=r_win.at[member, n],
            device_id=device(to),
            device_id_type=pl.DeviceIdType.MESH,
        )

    def back_copy(src, dst, send, recv, n, to):
        j = SLOTS[n]
        return pltpu.make_async_remote_copy(
            src_ref=src.at[rows(j)],
            dst_ref=dst.at[rows(j)],
            send_sem=send.at[n],
            recv_sem=recv.at[n],
            device_id=device(to),
            device_id_type=pl.DeviceIdType.MESH,
        )

    def stat_copy(d, to):
        n = others.index(d)
        return pltpu.make_async_remote_copy(
            src_ref=stat.at[REACH],
            dst_ref=stat.at[REACH - d],
            send_sem=s_stat.at[n],
            recv_sem=r_stat.at[n],
            device_id=device(to),
            device_id_type=pl.DeviceIdType.MESH,
        )

    even = lax.rem(me, 2) == 0

    def win_each(members, action, slots=range(len(SLOTS))):
        for member in members:
            for n in slots:
                j = SLOTS[n]
                other = me + j - R if action == "wait_recv" else me + R - j
                go = valid(other)
                if action != "wait_recv" and j == 0:
                    go = jnp.logical_and(go, even)
                if action != "wait_recv" and j == SPAN - 1:
                    go = jnp.logical_and(go, jnp.logical_not(even))

                @pl.when(go)
                def _():
                    getattr(win_copy(member, n, other), action)()

    def pass_on(members, action):
        for member in members:
            for parity, near, n, spare, step in ((0, 1, 0, 3, 1), (1, 3, 3, 0, -1)):
                go = jnp.logical_and(valid(me - step), valid(me + step))

                @pl.when(jnp.logical_and(go, lax.rem(me, 2) == parity))
                def _():
                    copy = pltpu.make_async_remote_copy(
                        src_ref=win.at[member, rows(near)],
                        dst_ref=win.at[member, rows(SLOTS[n])],
                        send_sem=s_win.at[member, spare],
                        recv_sem=r_win.at[member, n],
                        device_id=device(me + step),
                        device_id_type=pl.DeviceIdType.MESH,
                    )
                    getattr(copy, action)()

    def win_arrive(members):
        win_each(members, "wait_recv", (1, 2))
        pass_on(members, "start")
        win_each(members, "wait_recv", (0, 3))

    def back_each(src, dst, send, recv, action):
        for n, j in enumerate(SLOTS):
            other = me + R - j if action == "wait_recv" else me + j - R

            @pl.when(valid(other))
            def _():
                getattr(back_copy(src, dst, send, recv, n, other), action)()

    def gr_each(members, action, merged=None):
        for member in members:
            for n, j in enumerate(SLOTS):
                other = me + R - j if action == "wait_recv" else me + j - R
                for parity in (0, 1):
                    if j == 0 and parity or j == SPAN - 1 and not parity:
                        continue
                    if merged is not None and merged != ((j, parity) in ((1, 0), (3, 1))):
                        continue

                    @pl.when(jnp.logical_and(valid(other), lax.rem(me, 2) == parity))
                    def _():
                        copy = back_copy(
                            gr.at[member], gr_in.at[member], s_gr.at[member], r_gr.at[member], n, other
                        )
                        getattr(copy, action)()

    def hand_each(members, action):
        for member in members:
            for parity, j, step in ((0, SPAN - 1, 1), (1, 0, -1)):
                if action == "wait_recv":
                    go = jnp.logical_and(valid(me + step), valid(me - step))
                else:
                    go = jnp.logical_and(valid(me + 2 * step), valid(me + step))

                @pl.when(jnp.logical_and(go, lax.rem(me, 2) == parity))
                def _():
                    copy = pltpu.make_async_remote_copy(
                        src_ref=gr.at[member, rows(j)],
                        dst_ref=hand.at[member],
                        send_sem=s_hand.at[member],
                        recv_sem=r_hand.at[member],
                        device_id=device(me + step),
                        device_id_type=pl.DeviceIdType.MESH,
                    )
                    getattr(copy, action)()
                    if action == "wait_recv":
                        near = rows(1 if parity == 0 else 3)
                        both = gr[member, near, :].astype(f32) + hand[member].astype(f32)
                        gr[member, near, :] = both.astype(bf16)

    def stat_each(action):
        for d in others:
            other = me - d if action == "wait_recv" else me + d

            @pl.when(valid(other))
            def _():
                getattr(stat_copy(d, other), action)()

    win_each((AUDIO_Q, AUDIO_DOUT, AUDIO_K, AUDIO_V), "start")

    for j in SLOTS:

        @pl.when(jnp.logical_not(valid(me + j - R)))
        def _():
            for member in range(4):
                win[member, rows(j), :] = jnp.zeros((arows, hd), bf16)

        @pl.when(jnp.logical_not(valid(me + R - j)))
        def _():
            po_in[rows(j), :] = jnp.zeros((arows, hd), bf16)
            for member in range(3):
                gr_in[member, rows(j), :] = jnp.zeros((arows, hd), bf16)

    for parity, j in ((0, SPAN - 1), (1, 0)):

        @pl.when(lax.rem(me, 2) == parity)
        def _():
            for member in range(3):
                gr_in[member, rows(j), :] = jnp.zeros((arows, hd), bf16)

    empty = jnp.where(lax.broadcasted_iota(jnp.int32, (48, DH), 0) < 16, -HUGE, 0.0)
    stat[REACH] = empty
    for d in others:

        @pl.when(jnp.logical_not(valid(me - d)))
        def _():
            stat[REACH - d] = empty

    for load in loads[5:]:
        load.wait()
    lane_slot = lax.broadcasted_iota(jnp.int32, (1, wrows), 1) // arows
    linked_row = jnp.zeros((1, wrows), jnp.int32)
    for j in range(SPAN):
        on = link[0, j]
        bias[rows(j), :] = jnp.zeros((arows, vrows), f32) + jnp.where(on > 0, 0.0, -HUGE)
        linked_row = jnp.where(lane_slot == j, on, linked_row)
    linked_row = linked_row > 0

    def video_prepare(h, _):
        hs = lanes(h)
        for src, dst, keep, g in ((vq, qv, rq, 0), (vk, kv, rk, 1)):
            x = src[:, hs].astype(f32)
            rinv = rinv_of(x)
            keep[:, hs] = jnp.broadcast_to(rinv, (vrows, DH))
            y = turn(x, rinv, gain[g : g + 1, hs], tab_v[0, 0:1], tab_v[1, 0:1])
            dst[:, hs] = y.astype(bf16)
        return 0

    lax.fori_loop(0, heads, video_prepare, 0, unroll=4)

    win_arrive((AUDIO_Q, AUDIO_DOUT))

    def audio_forward(h, _):
        hs = lanes(h)
        v = vv[:, hs]
        r = nt(kv[:, hs], win[AUDIO_Q, :, hs]) * SCALE
        top = jnp.max(r, axis=0, keepdims=True)
        e = jnp.exp(r - top)
        ea[h] = e
        dp = nt(v, win[AUDIO_DOUT, :, hs])
        dpa[h] = dp
        stat[REACH, pl.ds(h, 1), 0:wrows] = jnp.where(linked_row, top, -HUGE)
        stat[REACH, pl.ds(16 + h, 1), 0:wrows] = jnp.where(
            linked_row, jnp.sum(e, axis=0, keepdims=True), 0.0
        )
        stat[REACH, pl.ds(32 + h, 1), 0:wrows] = jnp.where(
            linked_row, jnp.sum(e * dp, axis=0, keepdims=True), 0.0
        )
        po[:, hs] = tn(e.astype(bf16), v).astype(bf16)
        return 0

    lax.fori_loop(0, heads, audio_forward, 0, unroll=4)
    stat_each("start")
    back_each(po, po_in, s_po, r_po, "start")

    win_arrive((AUDIO_K, AUDIO_V))

    def video_side(h, _):
        hs = lanes(h)
        ka, va = win[AUDIO_K, :, hs], win[AUDIO_V, :, hs]
        q, do = qv[:, hs], vdo[:, hs]
        sc = nt(ka, q) * SCALE + bias[...]
        top = jnp.max(sc, axis=0, keepdims=True)
        e = jnp.exp(sc - top)
        p = e * (1.0 / jnp.sum(e, axis=0, keepdims=True))
        pb = p.astype(bf16)
        o_v[:, hs] = tn(pb, va).astype(bf16)
        dp = nt(va, do)
        delta = jnp.sum(p * dp, axis=0, keepdims=True)
        gs = (p * (dp - delta)).astype(bf16)
        gr[D_KEY, :, hs] = (nn(gs, q) * SCALE).astype(bf16)
        gr[D_VALUE, :, hs] = nn(pb, do).astype(bf16)
        dq = tn(gs, ka) * SCALE
        g_vq[:, hs] = turn_back(
            dq, vq[:, hs].astype(f32), rq[:, hs], gain[0:1, hs], tab_v[0, 0:1], tab_v[1, 0:1]
        ).astype(bf16)
        return 0

    lax.fori_loop(0, heads, video_side, 0, unroll=4)
    hand_each((D_KEY, D_VALUE), "start")
    gr_each((D_KEY, D_VALUE), "start", merged=False)

    hand_each((D_KEY, D_VALUE), "wait_recv")
    gr_each((D_KEY, D_VALUE), "start", merged=True)
    stat_each("wait_recv")
    lane = lax.broadcasted_iota(jnp.int32, (16, DH), 1)
    tops, totals, dots = [], [], []
    for t in range(2 * REACH + 1):
        shift = (t - REACH) * arows
        inside = jnp.logical_and(lane >= shift, lane < shift + wrows)
        rolled = [
            pltpu.roll(stat[t, 16 * i : 16 * i + 16], shift % DH, 1) if shift else stat[t, 16 * i : 16 * i + 16]
            for i in range(3)
        ]
        tops.append(jnp.where(inside, rolled[0], -HUGE))
        totals.append(jnp.where(inside, rolled[1], 0.0))
        dots.append(jnp.where(inside, rolled[2], 0.0))
    best = functools.reduce(jnp.maximum, tops)
    factors = [jnp.where(a > -0.5 * HUGE, jnp.exp(a - best), 0.0) for a in tops]
    total = sum(a * b for a, b in zip(factors, totals))
    inverse = 1.0 / jnp.where(total > 0.0, total, 1.0)
    coef[0] = factors[REACH] * inverse
    coef[1] = sum(a * b for a, b in zip(factors, dots)) * inverse
    wts[...] = jnp.zeros(wts.shape, f32)
    for j in range(SPAN):
        wts[16 * j : 16 * j + 16, :] = factors[REACH + R - j] * inverse

    def audio_back(h, _):
        hs = lanes(h)
        p = ea[h] * coef[0, pl.ds(h, 1), 0:wrows]
        ga = (p * (dpa[h] - coef[1, pl.ds(h, 1), 0:wrows])).astype(bf16)
        pab[h] = p.astype(bf16)
        gab[h] = ga
        gr[D_QUERY, :, hs] = (tn(ga, kv[:, hs]) * SCALE).astype(bf16)
        return 0

    lax.fori_loop(0, heads, audio_back, 0, unroll=4)
    hand_each((D_QUERY,), "start")
    gr_each((D_QUERY,), "start", merged=False)

    def video_back(h, _):
        hs = lanes(h)
        g_vv[:, hs] = nn(pab[h], win[AUDIO_DOUT, :, hs]).astype(bf16)
        dk = nn(gab[h], win[AUDIO_Q, :, hs]) * SCALE
        g_vk[:, hs] = turn_back(
            dk, vk[:, hs].astype(f32), rk[:, hs], gain[1:2, hs], tab_v[0, 0:1], tab_v[1, 0:1]
        ).astype(bf16)
        return 0

    lax.fori_loop(0, heads // 3, video_back, 0, unroll=4)
    hand_each((D_QUERY,), "wait_recv")
    gr_each((D_QUERY,), "start", merged=True)
    lax.fori_loop(heads // 3, heads, video_back, 0, unroll=4)

    turned = jnp.transpose(wts[...])[R * arows : (R + 1) * arows, :]
    back_each(po, po_in, s_po, r_po, "wait_recv")
    for h in range(heads):
        hs = slice(h * DH, (h + 1) * DH)
        acc = jnp.zeros((arows, DH), f32)
        for j in range(SPAN):
            part = (po if j == R else po_in)[j * arows : (j + 1) * arows, hs].astype(f32)
            acc += turned[:, 16 * j + h : 16 * j + h + 1] * part
        o_a[:, hs] = acc.astype(bf16)

    def merged(member, hs):
        acc = gr[member, rows(R), hs].astype(f32)
        for j in SLOTS:
            acc += gr_in[member, rows(j), hs].astype(f32)
        return acc

    def audio_grad(src, member, g, dst):
        def body(h, _):
            hs = lanes(h)
            x = src[:, hs].astype(f32)
            dst[:, hs] = turn_back(
                merged(member, hs), x, rinv_of(x), gain[g : g + 1, hs], tab_a[0], tab_a[1]
            ).astype(bf16)
            return 0

        lax.fori_loop(0, heads, body, 0, unroll=4)

    gr_each((D_KEY, D_VALUE), "wait_recv")
    g_av[...] = merged(D_VALUE, slice(None)).astype(bf16)
    audio_grad(ak, D_KEY, 3, g_ak)
    gr_each((D_QUERY,), "wait_recv")
    audio_grad(aq, D_QUERY, 2, g_aq)

    win_each(range(4), "wait_send")
    pass_on(range(4), "wait_send")
    stat_each("wait_send")
    back_each(po, po_in, s_po, r_po, "wait_send")
    hand_each(range(3), "wait_send")
    gr_each(range(3), "wait_send")


def write_out(*refs):
    n = len(refs) // 2
    sems = refs[-1]
    copies = [pltpu.make_async_copy(refs[i], refs[n + i], sems.at[i]) for i in range(n)]
    for copy in copies:
        copy.start()
    for copy in copies:
        copy.wait()


def on_device(along, count, *args):
    vq, aq = args[0], args[3]
    vrows, hd = vq.shape
    arows = aq.shape[0]
    heads = hd // DH
    wrows = SPAN * arows
    video = jax.ShapeDtypeStruct((vrows, hd), bf16)
    audio = jax.ShapeDtypeStruct((arows, hd), bf16)
    vmem = pl.BlockSpec(memory_space=pltpu.VMEM)
    dma = pltpu.SemaphoreType.DMA
    n = len(SLOTS)
    scratch = [
        pltpu.VMEM((4, wrows, hd), bf16),
        pltpu.VMEM((wrows, hd), bf16),
        pltpu.VMEM((wrows, hd), bf16),
        pltpu.VMEM((3, wrows, hd), bf16),
        pltpu.VMEM((3, wrows, hd), bf16),
        pltpu.VMEM((2 * REACH + 1, 48, DH), f32),
        pltpu.VMEM((vrows, hd), bf16),
        pltpu.VMEM((vrows, hd), bf16),
        pltpu.VMEM((heads, vrows, wrows), f32),
        pltpu.VMEM((heads, vrows, wrows), f32),
        pltpu.VMEM((heads, vrows, wrows), bf16),
        pltpu.VMEM((heads, vrows, wrows), bf16),
        pltpu.VMEM((vrows, hd), f32),
        pltpu.VMEM((vrows, hd), f32),
        pltpu.VMEM((2, 8, DH), f32),
        pltpu.VMEM((2, arows, DH), f32),
        pltpu.VMEM((2, 16, DH), f32),
        pltpu.VMEM((wrows, vrows), f32),
        pltpu.VMEM((DH, DH), f32),
        pltpu.VMEM((vrows, hd), bf16),
        pltpu.VMEM((vrows, hd), bf16),
        pltpu.VMEM((vrows, hd), bf16),
        pltpu.VMEM((arows, hd), bf16),
        pltpu.VMEM((arows, hd), bf16),
        pltpu.VMEM(args[6].shape, f32),
        pltpu.VMEM((vrows, hd), bf16),
        pltpu.SMEM(args[9].shape, jnp.int32),
        dma((10,)),
        dma((4, n)), dma((4, n)),
        dma((2 * REACH,)), dma((2 * REACH,)),
        dma((n,)), dma((n,)),
        dma((3, n)), dma((3, n)),
        pltpu.VMEM((3, arows, hd), bf16),
        dma((3,)), dma((3,)),
    ]
    results = pl.pallas_call(
        functools.partial(kernel, along, count),
        out_shape=[video, audio, video, video, video, audio, audio, audio],
        in_specs=[pl.BlockSpec(memory_space=pl.ANY)] * 10,
        out_specs=[vmem] * 8,
        scratch_shapes=scratch,
        compiler_params=pltpu.CompilerParams(
            collective_id=0, has_side_effects=True, vmem_limit_bytes=56 * 1024 * 1024
        ),
        name="linked_attention",
    )(*args)
    return pl.pallas_call(
        write_out,
        out_shape=[video, audio, video, video, video, audio, audio, audio],
        in_specs=[vmem] * 8,
        out_specs=[pl.BlockSpec(memory_space=pl.ANY)] * 8,
        scratch_shapes=[dma((8,))],
        name="write_out",
    )(*results)


def solution(mesh):
    along = mesh.shape["audio"]
    count = mesh.shape["video"] * along
    rows = P(("clips", "video", "audio"), None)
    return jax.shard_map(
        functools.partial(on_device, along, count),
        mesh=mesh,
        in_specs=(rows,) * 6 + (P(),) + (rows,) * 3,
        out_specs=(rows,) * 8,
        check_vma=False,
    )
```
